32 devices in a mesh: grp: 2 (over y), dev: 8 (over z, core), pool: 2 (over x).
Axes of the slice: x: 2, y: 2, z: 4, core: 2. Of those that a mesh axis runs over, the one named last changes fastest.
Arguments:
- hidden_in: bfloat16 [32, 2880], P(('grp', 'pool'), 'dev'), parts along dimension 0, may hold values from -4 to 4
- queries: bfloat16 [32, 8, 512], P(('grp', 'dev'), 'pool'), parts along dimension 0, may hold values from -40 to 40
- new_keyval: bfloat16 [32, 8, 128], P(('grp', 'dev'), 'pool'), parts along dimension 0, may hold values from -4 to 4
- cache_entries: bfloat16 [320, 2048, 128], P(('grp', 'dev', 'pool')), parts along dimension 0, may hold values from -4 to 4
- slot_table: int32 [32, 8], P('grp'), parts along dimension 0, may hold values from 0 to 159, as said below
- context_len: int32 [32], P('grp'), parts along dimension 0, may hold values from 1 to 2048, 16384 in all
- out_proj: bfloat16 [4096, 2880], P('pool', 'dev'), may hold values from -0.09375 to 0.09375
- norm_gain: float32 [2880], replicated, may hold values from 0.5 to 1.5
- expert_ids: int32 [32, 4], P('grp'), parts along dimension 0, may hold values from 0 to 7, all different within a row; in each aligned block of 16 rows (0 to 15, 16 to 31, ...) at most 16 rows name the same one
- expert_gates: float32 [32, 4], P('grp'), parts along dimension 0, may hold values from 0.05 to 0.5
- expert_in: bfloat16 [8, 2880, 2, 2880], P('dev', None, None, 'pool'), may hold values from -0.109375 to 0.109375
- expert_down: bfloat16 [8, 2880, 2880], P('dev', 'pool'), may hold values from -0.109375 to 0.109375
Outputs:
- hidden_out: bfloat16 [32, 2880], P(('grp', 'pool'), 'dev'), parts along dimension 0
The draws below stay inside these ranges and needn't reach their ends.
There are 2 independent parts, one for each index of `grp`. The reference program is written for one: setup_inputs(seed, part) draws one part's arguments, and reference() takes and returns one part's arrays. A program takes and returns all parts, laid end to end along the dimension named above; an argument that names none is the same for every part. Nothing has to cross between parts.
Inputs may be any that keep to these rules, and one draw needn't show every extreme that they name: `slot_table`: no two request-heads share a slot. The slot of request r and kv head h lies on the device of flat index slot // 10, counted with dev major and pool minor, and the pool index of that device is h // 4. `expert_ids`: each request names 4 different experts; no expert is named by more than 16 requests.
All inputs are finite; a program needn't handle non-finite values.
Results may differ from the reference program's by a relative error of at most 0.012.
Values may be sent and summed in bfloat16 or wider, within the bound.
A program may use at most 128 MiB of HBM per device.

```python
import math
import jax
import jax.numpy as jnp
import numpy as np
from jax import lax

D = 2880
FFH = 2880
HD = 64
QH = 64
KVH = 8
TOPK = 4
CTX = 2048
E = 8
QPK = 8
HPP = 4
B = 16
SLOT_DEV = 10
COLUMN_SLOTS = 80
SLOTS = 160
CAP = 16


def make_table(key):
    pools = KVH // HPP
    items = B * HPP

    def one_pool(pool_number):
        pool_key = jax.random.fold_in(jax.random.fold_in(key, 23), pool_number)
        inner = jax.random.permutation(jax.random.fold_in(pool_key, 1), jnp.arange(1, COLUMN_SLOTS - 1, dtype=jnp.int32))
        chosen = jnp.concatenate([jnp.array([0, COLUMN_SLOTS - 1], dtype=jnp.int32), inner])[:items]
        chosen = jax.random.permutation(jax.random.fold_in(pool_key, 2), chosen)
        device_row = chosen // SLOT_DEV
        within = chosen % SLOT_DEV
        return (device_row * pools + pool_number) * SLOT_DEV + within
    table = jax.vmap(one_pool)(jnp.arange(pools, dtype=jnp.int32))
    return table.reshape(pools, B, HPP).transpose(1, 0, 2).reshape(B, KVH)


def draw_slot_table(key, part):
    return make_table(key)


def draw_queries(key, part):
    shape = (B, KVH, QPK * HD)
    values = jnp.clip(jax.random.normal(jax.random.fold_in(key, 31), shape, jnp.float32), -6.0, 6.0)
    return values.astype(jnp.bfloat16)


def draw_new_keyval(key, part):
    shape = (B, KVH, 2 * HD)
    values = jnp.clip(jax.random.normal(jax.random.fold_in(key, 41), shape, jnp.float32), -4.0, 4.0)
    return values.astype(jnp.bfloat16)


def draw_cache_entries(key, part):
    shape = (SLOTS, CTX, 2 * HD)
    values = jnp.clip(jax.random.normal(jax.random.fold_in(key, 53), shape, jnp.float32), -4.0, 4.0)
    return values.astype(jnp.bfloat16)


def steps_of(key, dims, shards, smallest, high):
    level, own = 1.0, jax.random.fold_in(key, 6)
    for axis_at, blocks in shards:
        steps = jnp.exp(jax.random.uniform(jax.random.fold_in(own, axis_at), (blocks,), jnp.float32, smallest / len(shards), high / len(shards)))
        level = level * jnp.repeat(steps, dims[axis_at] // blocks).reshape([-1 if axis == axis_at else 1 for axis in range(len(dims))])
    return level


def profile(count, total, most, slope):
    loads = [(1 << 20) // math.isqrt(standing ** slope) + 1 for standing in range(2, count + 1)]
    rest, counts = total - most - (count - 1), [1] * (count - 1)
    while rest > 0:
        movable = [i for i in range(count - 1) if counts[i] < most]
        pool, left = sum([loads[i] for i in movable]), rest
        for i in movable:
            extra = min(most - counts[i], max(1, left * loads[i] // pool), rest)
            counts[i] = counts[i] + extra
            rest = rest - extra
    return np.array([most] + counts)


def ragged(stream_key, number_of, total, most, skew):
    if number_of == 2:
        one = jax.random.randint(stream_key, (), max(1, total - most), min(most, total - 1) + 1)
        return jnp.stack([one, total - one])
    lengths = jnp.asarray(profile(number_of, total, most, skew), jnp.int32)
    twos = (number_of - 1) // 2
    source_of, receiver = lengths[1:1 + 2 * twos:2], lengths[2:2 + 2 * twos:2]
    room = jnp.minimum(source_of - 1, most - receiver)
    shifted = jax.random.randint(jax.random.fold_in(stream_key, 1), (twos,), 0, 1 << 20) % (room + 1)
    lengths = lengths.at[1:1 + 2 * twos:2].set(source_of - shifted).at[2:2 + 2 * twos:2].set(receiver + shifted)
    return lengths[jax.random.permutation(jax.random.fold_in(stream_key, 2), number_of)]


def shared_out(key, own, number, rows, number_of, top, reach, lean):
    order = jax.random.permutation(key, number_of)
    heavy_load, ordinary = portions_of(number_of, rows * top, reach, lean, True), portions_of(number_of, rows * top, reach, lean, False)
    places = jnp.arange(number_of)

    def named(lengths, turn):
        used = int((lengths > 0).sum())
        fixed = max(1, used // 4)
        shifted = fixed + (places - fixed + turn * (used - fixed)) % max(1, number_of - fixed)
        return jnp.zeros((number_of,), jnp.int32).at[order[jnp.where(places < fixed, places, shifted)]].set(jnp.asarray(lengths, jnp.int32))

    lengths = jnp.where(number % 4 == 0, named(heavy_load, number // 4), named(ordinary, number - number // 4 - 1))
    mixed = jax.random.permutation(jax.random.fold_in(own, 3), number_of)
    donor, receiver = mixed[0:number_of // 2 * 2:2], mixed[1:number_of // 2 * 2:2]
    slack = jnp.minimum(lengths[donor] - 1, reach - lengths[receiver]) // 2
    slack = jnp.where((donor == order[0]) | (receiver == order[0]) | (lengths[receiver] == 0), 0, jnp.maximum(slack, 0))
    shifted = jax.random.randint(jax.random.fold_in(own, 4), (number_of // 2,), 0, 1 << 20) % (slack + 1)
    lengths = lengths.at[donor].add(-shifted).at[receiver].add(shifted)
    members = jnp.searchsorted(jnp.cumsum(lengths), jnp.arange(rows * top), side="right").astype(jnp.int32)
    grid = members.reshape(top, rows).T
    grid = grid[jax.random.permutation(jax.random.fold_in(own, 1), rows)]
    turn = jax.random.randint(jax.random.fold_in(own, 2), (rows, 1), 0, top)
    return jnp.take_along_axis(grid, (jnp.arange(top)[None, :] + turn) % top, axis=1)


def portions_of(amount, total, reach, lean, full):
    weights = [(1 << 20) // math.isqrt(standing ** lean) + 1 for standing in range(1, amount + 1)]
    largest = reach if full else min(reach, max(-(-total // amount), total * weights[0] // sum(weights)))
    least = 1 if total - largest >= amount - 1 else 0
    holding, rest = [largest] + [least] * (amount - 1), total - largest - least * (amount - 1)
    while rest > 0:
        free = [i for i in range(1, amount) if holding[i] < largest] or [i for i in range(1, amount) if holding[i] < reach]
        mass, left = sum([weights[i] for i in free]), rest
        for i in free:
            extra = min(reach - holding[i], max(1, left * weights[i] // mass), rest)
            holding[i] = holding[i] + extra
            rest = rest - extra
    return np.array(holding)


def scatter_about(stream_key, extent, width, most, shards=(), kind=jnp.bfloat16):
    entries = width * jax.random.normal(stream_key, extent, jnp.float32)
    if shards:
        entries = entries * steps_of(stream_key, extent, shards, -0.22, 0.18)
    return jnp.clip(entries, -most, most).astype(kind)


def setup_inputs(seed: int = 0, part: int = 0) -> dict:
    streams_of = jax.random.split(jax.random.key(seed), 13)
    part_keys = jax.random.split(jax.random.fold_in(streams_of[12], part), 13)
    hidden_in = scatter_about(part_keys[0], (B, D), 0.3, 4.0, ((0, 2), (1, 8)))
    queries = draw_queries(jax.random.fold_in(jax.random.fold_in(streams_of[12], part), 71), part)
    new_keyval = draw_new_keyval(jax.random.fold_in(jax.random.fold_in(streams_of[12], part), 71), part)
    cache_entries = draw_cache_entries(jax.random.fold_in(jax.random.fold_in(streams_of[12], part), 71), part)
    slot_table = draw_slot_table(jax.random.fold_in(jax.random.fold_in(streams_of[12], part), 71), part)
    context_len = ragged(part_keys[5], B, B * CTX // 2, CTX, 2).astype(jnp.int32)
    out_proj = scatter_about(streams_of[6], (QH * HD, D), (QH * HD) ** -0.5, 0.09375, ((0, 2), (1, 8)))
    norm_gain = jnp.clip(1.0 + 0.1 * jax.random.normal(streams_of[7], (D,), jnp.float32), 0.5, 1.5)
    expert_ids_keys = jax.random.split(jax.random.fold_in(part_keys[8], 1), B // B)
    expert_ids_turns = jax.random.permutation(jax.random.fold_in(part_keys[8], 3), B // B)
    expert_ids = jax.vmap(lambda own, number: shared_out(jax.random.fold_in(part_keys[8], 2), own, number, B, E, TOPK, CAP, 2))(expert_ids_keys, expert_ids_turns).reshape((B, TOPK))
    expert_gates = jnp.clip(jax.random.uniform(part_keys[9], (B, TOPK), jnp.float32, 0.05, 0.5), 0.05, 0.5)
    expert_in = scatter_about(streams_of[10], (E, D, 2, FFH), D ** -0.5, 0.109375, ((0, 8), (3, 2)))
    expert_down = scatter_about(streams_of[11], (E, FFH, D), FFH ** -0.5, 0.109375, ((0, 8), (1, 2)))
    return {"hidden_in": hidden_in, "queries": queries, "new_keyval": new_keyval, "cache_entries": cache_entries, "slot_table": slot_table, "context_len": context_len, "out_proj": out_proj, "norm_gain": norm_gain, "expert_ids": expert_ids, "expert_gates": expert_gates, "expert_in": expert_in, "expert_down": expert_down}


def request_attention(query_row, keyval_row, slot_row, length, cache_entries):
    chosen = cache_entries[slot_row]
    key_part = chosen[:, :, :HD].astype(jnp.float32)
    value_part = chosen[:, :, HD:].astype(jnp.float32)
    query_heads = query_row.reshape(KVH, QPK, HD).astype(jnp.float32)
    inv_root = 1.0 / math.sqrt(HD)
    scores = jnp.einsum('hgd,hcd->hgc', query_heads, key_part) * inv_root
    in_range = jnp.arange(CTX, dtype=jnp.int32) < length
    scores = jnp.where(in_range[None, None, :], scores, -1e+30)
    own_score = jnp.einsum('hgd,hd->hg', query_heads, keyval_row[:, :HD].astype(jnp.float32)) * inv_root
    highest = jnp.maximum(lax.optimization_barrier(jnp.max(scores, axis=2)), own_score)
    raised = jnp.exp(scores - highest[:, :, None])
    own_raised = jnp.exp(own_score - highest)
    denominator = lax.optimization_barrier(jnp.sum(raised, axis=2)) + own_raised
    probs_cache = (raised / denominator[:, :, None]).astype(jnp.bfloat16)
    probs_own = (own_raised / denominator).astype(jnp.bfloat16)
    mixed_out = jnp.einsum('hgc,hcd->hgd', probs_cache.astype(jnp.float32), value_part)
    mixed_out = mixed_out + probs_own.astype(jnp.float32)[:, :, None] * keyval_row[:, None, HD:].astype(jnp.float32)
    return mixed_out.astype(jnp.bfloat16).reshape(KVH * QPK * HD)

def reference(hidden_in, queries, new_keyval, cache_entries, slot_table, context_len, out_proj, norm_gain, expert_ids, expert_gates, expert_in, expert_down):

    def per_request(packed):
        return request_attention(packed[0], packed[1], packed[2], packed[3], cache_entries)
    attention = lax.map(per_request, (queries, new_keyval, slot_table, context_len))
    projected = jnp.dot(attention, out_proj, preferred_element_type=jnp.float32)
    residual = (hidden_in.astype(jnp.float32) + projected).astype(jnp.bfloat16)
    widened = residual.astype(jnp.float32)
    normed = (widened * lax.rsqrt(lax.optimization_barrier(jnp.mean(widened * widened, axis=1, keepdims=True)) + 1e-05) * norm_gain).astype(jnp.bfloat16)
    expert_index = jnp.arange(E, dtype=jnp.int32)
    route_weight = lax.optimization_barrier(jnp.sum(jnp.where(expert_ids[:, :, None] == expert_index[None, None, :], expert_gates[:, :, None], 0.0), axis=1))

    def one_expert(packed):
        weights_in, weights_down, column = packed
        both_parts = jnp.dot(normed, weights_in.reshape(D, 2 * FFH), preferred_element_type=jnp.float32)
        gate_part = both_parts[:, :FFH]
        up_part = both_parts[:, FFH:]
        activated = (gate_part * jax.nn.sigmoid(1.702 * gate_part) * (up_part + 1.0)).astype(jnp.bfloat16)
        return jnp.dot(activated, weights_down, preferred_element_type=jnp.float32) * column[:, None]
    expert_terms = lax.map(one_expert, (expert_in, expert_down, route_weight.T))
    mixture = lax.optimization_barrier(jnp.sum(expert_terms, axis=0))
    return (widened + mixture).astype(jnp.bfloat16)
```

```python
import functools
import math

import jax
import jax.numpy as jnp
from jax import lax
from jax.experimental import pallas as pl
from jax.experimental.pallas import tpu as pltpu
from jax.sharding import PartitionSpec as P

F32, BF16 = jnp.float32, jnp.bfloat16
NT = (((1,), (1,)), ((), ()))


def up_to(value, step):
    return -(-value // step) * step


def div(x, n):
    if n & (n - 1) == 0:
        return lax.shift_right_logical(x, jnp.full_like(x, n.bit_length() - 1))
    return lax.div(x, jnp.full_like(x, n))


def mod(x, n):
    if n & (n - 1) == 0:
        return x & (n - 1)
    return lax.rem(x, jnp.full_like(x, n))


def iota(shape, dim):
    return lax.broadcasted_iota(jnp.int32, shape, dim)


def pieces(rows):
    for count in (6, 5, 4, 3, 2):
        if rows % count == 0 and (rows // count) % 16 == 0:
            return count
    return 1


def dot(a, b):
    return jnp.dot(a, b, preferred_element_type=F32)


def dot_nt(a, b):
    return lax.dot_general(a, b, NT, preferred_element_type=F32)


def kernel(
    devs,
    pools,
    pool_heads,
    slots,
    col_block,
    hidden,
    pack,
    table_t,
    lengths,
    gain,
    ids_t,
    gates_t,
    cache_hbm,
    proj_hbm,
    in_hbm,
    down_hbm,
    out,
    cache,
    proj_w,
    in_w,
    down_w,
    g_query,
    g_attn,
    g_sum,
    g_resid,
    s_moe,
    g_moe,
    g_last,
    acc,
    cache_sem,
    proj_sem,
    in_sem,
    down_sem,
    dev_send,
    dev_recv,
    pool_send,
    pool_recv,
):
    me_d, me_p = lax.axis_index("dev"), lax.axis_index("pool")
    requests = table_t.shape[1]
    row_block = hidden.shape[0]
    head_dim = cache.shape[2] // 2
    pair = 2 * head_dim
    width = proj_w.shape[1] // pool_heads
    group = width // head_dim
    half_w = width // 2
    half_g = group // 2
    pack_rows = pack.shape[0]
    part = pack_rows // 2
    per_dev = requests // devs
    chunks = in_w.shape[1]
    inv_root = 1.0 / math.sqrt(head_dim)

    cache_copies = [
        pltpu.make_async_copy(cache_hbm.at[s], cache.at[s], cache_sem.at[s]) for s in range(slots)
    ]
    for copy in cache_copies:
        copy.start()
    proj_copy = pltpu.make_async_copy(proj_hbm, proj_w, proj_sem.at[0])
    proj_copy.start()

    def in_copy(part_at, c):
        return pltpu.make_async_copy(
            in_hbm.at[part_at, c], in_w.at[part_at, c], in_sem.at[part_at, c]
        )

    def down_copy(c):
        return pltpu.make_async_copy(down_hbm.at[c], down_w.at[c], down_sem.at[c])

    for c in range(chunks):
        in_copy(0, c).start()
        in_copy(1, c).start()
        down_copy(c).start()

    barrier = pltpu.get_barrier_semaphore()
    for axis, me, n in (("dev", me_d, devs), ("pool", me_p, pools)):
        for k in range(1, n):
            pl.semaphore_signal(
                barrier,
                inc=1,
                device_id={axis: lax.rem(me + k, n)},
                device_id_type=pl.DeviceIdType.MESH,
            )
    pl.semaphore_wait(barrier, devs + pools - 2)

    def exchange(axis, me, n, phase, dst, source=None):
        send, recv = (dev_send, dev_recv) if axis == "dev" else (pool_send, pool_recv)
        copies = []
        for k in range(1, n):
            peer = lax.rem(me + k, n)
            copies.append(
                pltpu.make_async_remote_copy(
                    src_ref=dst.at[me] if source is None else source.at[peer],
                    dst_ref=dst.at[me],
                    send_sem=send.at[phase, k - 1],
                    recv_sem=recv.at[phase, k - 1],
                    device_id={axis: peer},
                    device_id_type=pl.DeviceIdType.MESH,
                )
            )
            copies[-1].start()
        return copies

    def finish(copies):
        for copy in copies:
            copy.wait()

    g_query[me_d] = pack[...]
    sent = exchange("dev", me_d, devs, 0, g_query)

    table = table_t[...].astype(F32)
    rows = slots * group
    first = ((me_d * pools + me_p) * slots).astype(F32)
    row_id = div(iota((rows, 1), 0), group).astype(F32) + first
    len_row = lengths[...].astype(F32)
    cols = devs * pack_rows
    req_at, col_at = iota((requests, cols), 0), iota((requests, cols), 1)
    inner = mod(col_at, part)
    same_request = div(col_at, pack_rows) * per_dev + div(inner, pool_heads) == req_at
    length = jnp.zeros((rows, 1), F32)
    pick = jnp.zeros((rows, cols), F32)
    own_rows = []
    for h in range(pool_heads):
        line = jnp.zeros((1, requests), F32)
        for p in range(pools):
            at = p * pool_heads + h
            line = line + jnp.where(me_p == p, table[at : at + 1, :], 0.0)
        own_rows.append(line)
        mine = jnp.where(line == row_id, 1.0, 0.0)
        length = length + jnp.sum(mine * len_row, axis=1, keepdims=True)
        place = jnp.where(same_request & (mod(inner, pool_heads) == h), 1.0, 0.0)
        pick = pick + dot(mine.astype(BF16), place.astype(BF16))
    row_at, col_at = iota((rows, cols), 0), iota((rows, cols), 1)
    right_half = div(mod(col_at, pack_rows), part) == div(mod(row_at, group), half_g)
    pick = jnp.where(right_half, pick, 0.0).astype(BF16)
    own_g = div(iota((rows, half_w), 1), head_dim) == mod(iota((rows, half_w), 0), half_g)
    fold_at, fold_to = iota((half_w, pair), 0), iota((half_w, pair), 1)
    fold = jnp.where(mod(fold_at, head_dim) == fold_to, 1.0, 0.0).astype(BF16)
    diagonal = iota((requests, requests), 0) == iota((requests, requests), 1)

    def column(line):
        return jnp.sum(jnp.where(diagonal, line, 0.0), axis=1, keepdims=True)

    slot_rows = g_attn.shape[1]
    lane = iota((1, devs * slot_rows), 1)
    lane_slot = mod(lane, slot_rows)
    lane_id = ((div(lane, slot_rows) * pools + me_p) * slots + lane_slot).astype(F32)
    lane_id = jnp.where(lane_slot < slots, lane_id, -1.0)
    attn_picks = [
        jnp.where(column(line) == lane_id, 1.0, 0.0).astype(BF16) for line in own_rows
    ]
    gate_line = jnp.sum(
        jnp.where(ids_t[...] == me_d, gates_t[...], 0.0), axis=0, keepdims=True
    )
    route = column(gate_line)

    finish(sent)
    spread = dot(pick, g_query[...].reshape(cols, g_query.shape[2]))
    query = dot(jnp.where(own_g, spread[:, :half_w], 0.0).astype(BF16), fold)
    fresh = spread[:, half_w : half_w + pair]
    own_score = jnp.sum(query * fresh, axis=1, keepdims=True) * inv_root

    mixed = []
    position = iota((group, cache.shape[1]), 1).astype(F32)
    for s in range(slots):
        cache_copies[s].wait()
        at = slice(s * group, (s + 1) * group)
        entries = cache[s]
        scores = dot_nt(query[at].astype(BF16), entries) * inv_root
        scores = jnp.where(position < length[at], scores, -1e30)
        highest = jnp.maximum(jnp.max(scores, axis=1, keepdims=True), own_score[at])
        raised = jnp.exp(scores - highest)
        own_raised = jnp.exp(own_score[at] - highest)
        scale = 1.0 / (jnp.sum(raised, axis=1, keepdims=True) + own_raised)
        probs = (raised * scale).astype(BF16)
        own_prob = (own_raised * scale).astype(BF16).astype(F32)
        mixed.append(dot(probs, entries) + own_prob * fresh[at])
    mixed = jnp.concatenate(mixed, axis=0)
    values = mixed[:, head_dim:]
    twice = jnp.concatenate([values, values], axis=1)
    wide = jnp.concatenate([twice] * (group // 2), axis=1)
    own_block = div(iota((rows, width), 1), head_dim) == mod(iota((rows, width), 0), group)
    wide = jnp.where(own_block, wide, 0.0).astype(BF16)
    gather = jnp.where(
        div(iota((slot_rows, rows), 1), group) == iota((slot_rows, rows), 0), 1.0, 0.0
    ).astype(BF16)
    g_attn[me_d] = dot(gather, wide).astype(BF16)

    finish_attn = exchange("dev", me_d, devs, 1, g_attn)
    hidden_rows = hidden[...].astype(F32)
    partial = jnp.concatenate(
        [jnp.where(me_p == p, hidden_rows, 0.0) for p in range(pools)], axis=0
    )
    proj_copy.wait()
    finish(finish_attn)
    all_attn = g_attn[...].reshape(devs * slot_rows, width)
    for h in range(pool_heads):
        chosen = dot(attn_picks[h], all_attn).astype(BF16)
        partial = partial + dot_nt(chosen, proj_w[:, h * width : (h + 1) * width])

    pad = g_sum.shape[2] - col_block

    def padded(x):
        if not pad:
            return x
        return jnp.concatenate([x, jnp.zeros((x.shape[0], pad), x.dtype)], axis=1)

    g_sum[me_p] = padded(partial)
    finish(exchange("pool", me_p, pools, 0, g_sum))
    total = g_sum[0]
    for p in range(1, pools):
        total = total + g_sum[p]
    g_resid[me_d] = total.astype(BF16)

    finish(exchange("dev", me_d, devs, 2, g_resid))
    full = jnp.concatenate(
        [g_resid[d].astype(F32)[:, :col_block] for d in range(devs)], axis=1
    )
    mean = jnp.sum(full * full, axis=1, keepdims=True) * (1.0 / full.shape[1])
    normed = (full * lax.rsqrt(mean + 1e-05) * gain[...]).astype(BF16)

    acc[...] = jnp.zeros_like(acc)

    def expert(c, carry):
        in_copy(0, c).wait()
        in_copy(1, c).wait()
        gate = dot_nt(normed, in_w[0, c])
        up = dot_nt(normed, in_w[1, c])
        act = (gate * jax.nn.sigmoid(1.702 * gate) * (up + 1.0)).astype(BF16)
        down_copy(c).wait()
        acc[...] += dot(act, down_w[c])
        return carry

    lax.fori_loop(0, chunks, expert, 0)
    terms = acc[...] * route
    for d in range(devs):
        s_moe[d] = padded(terms[:, d * col_block : (d + 1) * col_block]).astype(BF16)
    g_moe[me_d] = s_moe[me_d]
    finish(exchange("dev", me_d, devs, 3, g_moe, s_moe))
    summed = g_moe[0].astype(F32)
    for d in range(1, devs):
        summed = summed + g_moe[d].astype(F32)
    g_last[me_p] = summed
    finish(exchange("pool", me_p, pools, 1, g_last))
    summed = g_last[0]
    for p in range(1, pools):
        summed = summed + g_last[p]
    result = summed + g_resid[me_d].astype(F32)
    mine = jnp.zeros((row_block, result.shape[1]), F32)
    for p in range(pools):
        mine = mine + jnp.where(me_p == p, result[p * row_block : (p + 1) * row_block], 0.0)
    out[...] = mine[:, :col_block].astype(BF16)


def body(
    devs,
    pools,
    hidden_in,
    queries,
    new_keyval,
    cache_entries,
    slot_table,
    context_len,
    out_proj,
    norm_gain,
    expert_ids,
    expert_gates,
    expert_in,
    expert_down,
):
    slots, context, pair = cache_entries.shape
    requests = slot_table.shape[0]
    pool_heads, width = queries.shape[1:]
    features = norm_gain.shape[0]
    hidden_units = expert_down.shape[1]
    col_block = hidden_in.shape[1]
    col_pad = up_to(col_block, 128)
    part = queries.shape[0] * pool_heads
    chunks = pieces(hidden_units)
    q = queries.reshape(part, width)
    kv = new_keyval.reshape(part, pair)
    pack = jnp.concatenate(
        [
            jnp.concatenate([q[:, : width // 2], kv], axis=1),
            jnp.concatenate([q[:, width // 2 :], kv], axis=1),
        ],
        axis=0,
    )
    slot_rows = up_to(slots, 16)
    depth = hidden_units // chunks
    vmem = pl.BlockSpec(memory_space=pltpu.VMEM)
    hbm = pl.BlockSpec(memory_space=pl.ANY)
    dma = pltpu.SemaphoreType.DMA
    return pl.pallas_call(
        functools.partial(kernel, devs, pools, pool_heads, slots, col_block),
        out_shape=jax.ShapeDtypeStruct(hidden_in.shape, BF16),
        in_specs=[vmem] * 7 + [hbm] * 4,
        out_specs=vmem,
        scratch_shapes=[
            pltpu.VMEM((slots, context, pair), BF16),
            pltpu.VMEM((out_proj.shape[1], out_proj.shape[0]), BF16),
            pltpu.VMEM((2, chunks, depth, features), BF16),
            pltpu.VMEM((chunks, depth, features), BF16),
            pltpu.VMEM((devs,) + pack.shape, BF16),
            pltpu.VMEM((devs, slot_rows, width), BF16),
            pltpu.VMEM((pools, requests, col_pad), F32),
            pltpu.VMEM((devs, requests, col_pad), BF16),
            pltpu.VMEM((devs, requests, col_pad), BF16),
            pltpu.VMEM((devs, requests, col_pad), BF16),
            pltpu.VMEM((pools, requests, col_pad), F32),
            pltpu.VMEM((requests, features), F32),
            dma((slots,)),
            dma((1,)),
            dma((2, chunks)),
            dma((chunks,)),
            dma((4, devs - 1)),
            dma((4, devs - 1)),
            dma((2, pools - 1)),
            dma((2, pools - 1)),
        ],
        compiler_params=pltpu.CompilerParams(
            collective_id=0, has_side_effects=True, vmem_limit_bytes=58 * 2**20
        ),
    )(
        hidden_in,
        pack,
        slot_table.T,
        context_len.reshape(1, requests),
        norm_gain.reshape(1, features),
        expert_ids.T,
        expert_gates.T,
        cache_entries,
        out_proj.T,
        expert_in[0].transpose(1, 2, 0).reshape(2, chunks, depth, features),
        expert_down.reshape(chunks, depth, features),
    )


def solution(mesh):
    return jax.shard_map(
        functools.partial(body, mesh.shape["dev"], mesh.shape["pool"]),
        mesh=mesh,
        in_specs=(
            P(("grp", "pool"), "dev"),
            P(("grp", "dev"), "pool", None),
            P(("grp", "dev"), "pool", None),
            P(("grp", "dev", "pool"), None, None),
            P("grp", None),
            P("grp"),
            P("pool", "dev"),
            P(),
            P("grp", None),
            P("grp", None),
            P("dev", None, None, "pool"),
            P("dev", "pool", None),
        ),
        out_specs=P(("grp", "pool"), "dev"),
        check_vma=False,
    )
```

```python
import functools
import math

import jax
import jax.numpy as jnp
from jax import lax
from jax.experimental import pallas as pl
from jax.experimental.pallas import tpu as pltpu
from jax.sharding import PartitionSpec as P

F32, BF16 = jnp.float32, jnp.bfloat16
NT = (((1,), (1,)), ((), ()))


def up_to(value, step):
    return -(-value // step) * step


def div(x, n):
    if n & (n - 1) == 0:
        return lax.shift_right_logical(x, jnp.full_like(x, n.bit_length() - 1))
    return lax.div(x, jnp.full_like(x, n))


def mod(x, n):
    if n & (n - 1) == 0:
        return x & (n - 1)
    return lax.rem(x, jnp.full_like(x, n))


def iota(shape, dim):
    return lax.broadcasted_iota(jnp.int32, shape, dim)


def pieces(rows):
    for count in (6, 5, 4, 3, 2):
        if rows % count == 0 and (rows // count) % 16 == 0:
            return count
    return 1


def dot(a, b):
    return jnp.dot(a, b, preferred_element_type=F32)


def dot_nt(a, b):
    return lax.dot_general(a, b, NT, preferred_element_type=F32)


def kernel(
    devs,
    pools,
    pool_heads,
    slots,
    col_block,
    hidden,
    queries,
    new_keyval,
    table_t,
    lengths,
    gain,
    ids_t,
    gates_t,
    cache_hbm,
    proj_hbm,
    in_hbm,
    down_hbm,
    out,
    cache,
    proj_w,
    in_w,
    down_w,
    g_query,
    g_attn,
    g_sum,
    g_resid,
    s_moe,
    g_moe,
    g_last,
    acc,
    cache_sem,
    proj_sem,
    in_sem,
    down_sem,
    dev_send,
    dev_recv,
    pool_send,
    pool_recv,
):
    me_d, me_p = lax.axis_index("dev"), lax.axis_index("pool")
    requests = table_t.shape[1]
    row_block = hidden.shape[0]
    head_dim = cache.shape[2] // 2
    pair = 2 * head_dim
    width = proj_w.shape[1] // pool_heads
    group = width // head_dim
    half_w = width // 2
    half_g = group // 2
    pack_rows = g_query.shape[1]
    part = pack_rows // 2
    per_dev = requests // devs
    chunks = in_w.shape[1]
    inv_root = 1.0 / math.sqrt(head_dim)

    cache_copies = [
        pltpu.make_async_copy(cache_hbm.at[s], cache.at[s], cache_sem.at[s]) for s in range(slots)
    ]
    for copy in cache_copies:
        copy.start()
    proj_copy = pltpu.make_async_copy(proj_hbm, proj_w, proj_sem.at[0])
    proj_copy.start()

    def in_copy(part_at, c):
        return pltpu.make_async_copy(
            in_hbm.at[part_at, c], in_w.at[part_at, c], in_sem.at[part_at, c]
        )

    def down_copy(c):
        return pltpu.make_async_copy(down_hbm.at[c], down_w.at[c], down_sem.at[c])

    for c in range(chunks):
        in_copy(0, c).start()
        in_copy(1, c).start()
        down_copy(c).start()

    barrier = pltpu.get_barrier_semaphore()
    for axis, me, n in (("dev", me_d, devs), ("pool", me_p, pools)):
        for k in range(1, n):
            pl.semaphore_signal(
                barrier,
                inc=1,
                device_id={axis: lax.rem(me + k, n)},
                device_id_type=pl.DeviceIdType.MESH,
            )
    pl.semaphore_wait(barrier, devs + pools - 2)

    def exchange(axis, me, n, phase, dst, source=None):
        send, recv = (dev_send, dev_recv) if axis == "dev" else (pool_send, pool_recv)
        copies = []
        for k in range(1, n):
            peer = lax.rem(me + k, n)
            copies.append(
                pltpu.make_async_remote_copy(
                    src_ref=dst.at[me] if source is None else source.at[peer],
                    dst_ref=dst.at[me],
                    send_sem=send.at[phase, k - 1],
                    recv_sem=recv.at[phase, k - 1],
                    device_id={axis: peer},
                    device_id_type=pl.DeviceIdType.MESH,
                )
            )
            copies[-1].start()
        return copies

    def finish(copies):
        for copy in copies:
            copy.wait()

    count = queries.shape[0]
    q = jnp.concatenate([queries[i].astype(F32) for i in range(count)], axis=0)
    kv = jnp.concatenate([new_keyval[i].astype(F32) for i in range(count)], axis=0)
    left = jnp.concatenate([q[:, :half_w], kv], axis=1)
    right = jnp.concatenate([q[:, half_w:], kv], axis=1)
    g_query[me_d] = jnp.concatenate([left, right], axis=0).astype(BF16)
    sent = exchange("dev", me_d, devs, 0, g_query)

    table = table_t[...].astype(F32)
    rows = slots * group
    first = ((me_d * pools + me_p) * slots).astype(F32)
    row_id = div(iota((rows, 1), 0), group).astype(F32) + first
    len_row = lengths[...].astype(F32)
    cols = devs * pack_rows
    req_at, col_at = iota((requests, cols), 0), iota((requests, cols), 1)
    inner = mod(col_at, part)
    same_request = div(col_at, pack_rows) * per_dev + div(inner, pool_heads) == req_at
    length = jnp.zeros((rows, 1), F32)
    pick = jnp.zeros((rows, cols), F32)
    own_rows = []
    for h in range(pool_heads):
        line = jnp.zeros((1, requests), F32)
        for p in range(pools):
            at = p * pool_heads + h
            line = line + jnp.where(me_p == p, table[at : at + 1, :], 0.0)
        own_rows.append(line)
        mine = jnp.where(line == row_id, 1.0, 0.0)
        length = length + jnp.sum(mine * len_row, axis=1, keepdims=True)
        place = jnp.where(same_request & (mod(inner, pool_heads) == h), 1.0, 0.0)
        pick = pick + dot(mine.astype(BF16), place.astype(BF16))
    row_at, col_at = iota((rows, cols), 0), iota((rows, cols), 1)
    right_half = div(mod(col_at, pack_rows), part) == div(mod(row_at, group), half_g)
    pick = jnp.where(right_half, pick, 0.0).astype(BF16)
    own_g = div(iota((rows, half_w), 1), head_dim) == mod(iota((rows, half_w), 0), half_g)
    fold_at, fold_to = iota((half_w, pair), 0), iota((half_w, pair), 1)
    fold = jnp.where(mod(fold_at, head_dim) == fold_to, 1.0, 0.0).astype(BF16)
    diagonal = iota((requests, requests), 0) == iota((requests, requests), 1)

    def column(line):
        return jnp.sum(jnp.where(diagonal, line, 0.0), axis=1, keepdims=True)

    slot_rows = g_attn.shape[1]
    lane = iota((1, devs * slot_rows), 1)
    lane_slot = mod(lane, slot_rows)
    lane_id = ((div(lane, slot_rows) * pools + me_p) * slots + lane_slot).astype(F32)
    lane_id = jnp.where(lane_slot < slots, lane_id, -1.0)
    attn_picks = [
        jnp.where(column(line) == lane_id, 1.0, 0.0).astype(BF16) for line in own_rows
    ]
    gate_line = jnp.sum(
        jnp.where(ids_t[...] == me_d, gates_t[...], 0.0), axis=0, keepdims=True
    )
    route = column(gate_line)

    finish(sent)
    spread = dot(pick, g_query[...].reshape(cols, g_query.shape[2]))
    query = dot(jnp.where(own_g, spread[:, :half_w], 0.0).astype(BF16), fold)
    fresh = spread[:, half_w : half_w + pair]
    own_score = jnp.sum(query * fresh, axis=1, keepdims=True) * inv_root

    mixed = []
    position = iota((group, cache.shape[1]), 1).astype(F32)
    for s in range(slots):
        cache_copies[s].wait()
        at = slice(s * group, (s + 1) * group)
        entries = cache[s]
        scores = dot_nt(query[at].astype(BF16), entries) * inv_root
        scores = jnp.where(position < length[at], scores, -1e30)
        highest = jnp.maximum(jnp.max(scores, axis=1, keepdims=True), own_score[at])
        raised = jnp.exp(scores - highest)
        own_raised = jnp.exp(own_score[at] - highest)
        scale = 1.0 / (jnp.sum(raised, axis=1, keepdims=True) + own_raised)
        probs = (raised * scale).astype(BF16)
        own_prob = (own_raised * scale).astype(BF16).astype(F32)
        mixed.append(dot(probs, entries) + own_prob * fresh[at])
    mixed = jnp.concatenate(mixed, axis=0)
    values = mixed[:, head_dim:]
    twice = jnp.concatenate([values, values], axis=1)
    wide = jnp.concatenate([twice] * (group // 2), axis=1)
    own_block = div(iota((rows, width), 1), head_dim) == mod(iota((rows, width), 0), group)
    wide = jnp.where(own_block, wide, 0.0).astype(BF16)
    gather = jnp.where(
        div(iota((slot_rows, rows), 1), group) == iota((slot_rows, rows), 0), 1.0, 0.0
    ).astype(BF16)
    g_attn[me_d] = dot(gather, wide).astype(BF16)

    finish_attn = exchange("dev", me_d, devs, 1, g_attn)
    hidden_rows = hidden[...].astype(F32)
    partial = jnp.concatenate(
        [jnp.where(me_p == p, hidden_rows, 0.0) for p in range(pools)], axis=0
    )
    proj_copy.wait()
    finish(finish_attn)
    all_attn = g_attn[...].reshape(devs * slot_rows, width)
    for h in range(pool_heads):
        chosen = dot(attn_picks[h], all_attn).astype(BF16)
        partial = partial + dot_nt(chosen, proj_w[:, h * width : (h + 1) * width])

    pad = g_sum.shape[2] - col_block

    def padded(x):
        if not pad:
            return x
        return jnp.concatenate([x, jnp.zeros((x.shape[0], pad), x.dtype)], axis=1)

    g_sum[me_p] = padded(partial)
    finish(exchange("pool", me_p, pools, 0, g_sum))
    total = g_sum[0]
    for p in range(1, pools):
        total = total + g_sum[p]
    g_resid[me_d] = total.astype(BF16)

    finish(exchange("dev", me_d, devs, 2, g_resid))
    full = jnp.concatenate(
        [g_resid[d].astype(F32)[:, :col_block] for d in range(devs)], axis=1
    )
    mean = jnp.sum(full * full, axis=1, keepdims=True) * (1.0 / full.shape[1])
    normed = (full * lax.rsqrt(mean + 1e-05) * gain[...].reshape(1, -1)).astype(BF16)

    acc[...] = jnp.zeros_like(acc)

    def expert(c, carry):
        in_copy(0, c).wait()
        in_copy(1, c).wait()
        gate = dot_nt(normed, in_w[0, c])
        up = dot_nt(normed, in_w[1, c])
        act = (gate * jax.nn.sigmoid(1.702 * gate) * (up + 1.0)).astype(BF16)
        down_copy(c).wait()
        acc[...] += dot(act, down_w[c])
        return carry

    lax.fori_loop(0, chunks, expert, 0)
    terms = acc[...] * route
    for d in range(devs):
        s_moe[d] = padded(terms[:, d * col_block : (d + 1) * col_block]).astype(BF16)
    g_moe[me_d] = s_moe[me_d]
    finish(exchange("dev", me_d, devs, 3, g_moe, s_moe))
    summed = g_moe[0].astype(F32)
    for d in range(1, devs):
        summed = summed + g_moe[d].astype(F32)
    g_last[me_p] = summed
    finish(exchange("pool", me_p, pools, 1, g_last))
    summed = g_last[0]
    for p in range(1, pools):
        summed = summed + g_last[p]
    result = summed + g_resid[me_d].astype(F32)
    mine = jnp.zeros((row_block, result.shape[1]), F32)
    for p in range(pools):
        mine = mine + jnp.where(me_p == p, result[p * row_block : (p + 1) * row_block], 0.0)
    out[...] = mine[:, :col_block].astype(BF16)


def body(
    devs,
    pools,
    hidden_in,
    queries,
    new_keyval,
    cache_entries,
    slot_table,
    context_len,
    out_proj,
    norm_gain,
    expert_ids,
    expert_gates,
    expert_in,
    expert_down,
):
    slots, context, pair = cache_entries.shape
    requests = slot_table.shape[0]
    pool_heads, width = queries.shape[1:]
    features = norm_gain.shape[0]
    hidden_units = expert_down.shape[1]
    col_block = hidden_in.shape[1]
    col_pad = up_to(col_block, 128)
    part = queries.shape[0] * pool_heads
    chunks = pieces(hidden_units)
    slot_rows = up_to(slots, 16)
    depth = hidden_units // chunks
    vmem = pl.BlockSpec(memory_space=pltpu.VMEM)
    hbm = pl.BlockSpec(memory_space=pl.ANY)
    dma = pltpu.SemaphoreType.DMA
    return pl.pallas_call(
        functools.partial(kernel, devs, pools, pool_heads, slots, col_block),
        out_shape=jax.ShapeDtypeStruct(hidden_in.shape, BF16),
        in_specs=[vmem] * 8 + [hbm] * 4,
        out_specs=vmem,
        scratch_shapes=[
            pltpu.VMEM((slots, context, pair), BF16),
            pltpu.VMEM((out_proj.shape[1], out_proj.shape[0]), BF16),
            pltpu.VMEM((2, chunks, depth, features), BF16),
            pltpu.VMEM((chunks, depth, features), BF16),
            pltpu.VMEM((devs, 2 * part, width // 2 + pair), BF16),
            pltpu.VMEM((devs, slot_rows, width), BF16),
            pltpu.VMEM((pools, requests, col_pad), F32),
            pltpu.VMEM((devs, requests, col_pad), BF16),
            pltpu.VMEM((devs, requests, col_pad), BF16),
            pltpu.VMEM((devs, requests, col_pad), BF16),
            pltpu.VMEM((pools, requests, col_pad), F32),
            pltpu.VMEM((requests, features), F32),
            dma((slots,)),
            dma((1,)),
            dma((2, chunks)),
            dma((chunks,)),
            dma((4, devs - 1)),
            dma((4, devs - 1)),
            dma((2, pools - 1)),
            dma((2, pools - 1)),
        ],
        compiler_params=pltpu.CompilerParams(
            collective_id=0, has_side_effects=True, vmem_limit_bytes=58 * 2**20
        ),
    )(
        hidden_in,
        queries,
        new_keyval,
        slot_table.T,
        context_len.reshape(1, requests),
        norm_gain,
        expert_ids.T,
        expert_gates.T,
        cache_entries,
        out_proj.T,
        expert_in[0].transpose(1, 2, 0).reshape(2, chunks, depth, features),
        expert_down.reshape(chunks, depth, features),
    )


def solution(mesh):
    return jax.shard_map(
        functools.partial(body, mesh.shape["dev"], mesh.shape["pool"]),
        mesh=mesh,
        in_specs=(
            P(("grp", "pool"), "dev"),
            P(("grp", "dev"), "pool", None),
            P(("grp", "dev"), "pool", None),
            P(("grp", "dev", "pool"), None, None),
            P("grp", None),
            P("grp"),
            P("pool", "dev"),
            P(),
            P("grp", None),
            P("grp", None),
            P("dev", None, None, "pool"),
            P("dev", "pool", None),
        ),
        out_specs=P(("grp", "pool"), "dev"),
        check_vma=False,
    )
```

```python
import functools
import math

import jax
import jax.numpy as jnp
from jax import lax
from jax.experimental import pallas as pl
from jax.experimental.pallas import tpu as pltpu
from jax.sharding import PartitionSpec as P

F32, BF16 = jnp.float32, jnp.bfloat16
NT = (((1,), (1,)), ((), ()))


def up_to(value, step):
    return -(-value // step) * step


def div(x, n):
    if n & (n - 1) == 0:
        return lax.shift_right_logical(x, jnp.full_like(x, n.bit_length() - 1))
    return lax.div(x, jnp.full_like(x, n))


def mod(x, n):
    if n & (n - 1) == 0:
        return x & (n - 1)
    return lax.rem(x, jnp.full_like(x, n))


def iota(shape, dim):
    return lax.broadcasted_iota(jnp.int32, shape, dim)


def pieces(rows):
    for count in (6, 5, 4, 3, 2):
        if rows % count == 0 and (rows // count) % 16 == 0:
            return count
    return 1


def dot(a, b):
    return jnp.dot(a, b, preferred_element_type=F32)


def dot_nt(a, b):
    return lax.dot_general(a, b, NT, preferred_element_type=F32)


def kernel(
    devs,
    pools,
    pool_heads,
    slots,
    col_block,
    hidden,
    queries,
    new_keyval,
    table_t,
    lengths,
    gain,
    ids_t,
    gates_t,
    cache_hbm,
    proj_hbm,
    in_hbm,
    down_hbm,
    out,
    cache,
    proj_w,
    in_w,
    down_w,
    g_query,
    g_attn,
    g_sum,
    g_resid,
    s_moe,
    g_moe,
    acc,
    cache_sem,
    proj_sem,
    in_sem,
    down_sem,
    dev_send,
    dev_recv,
    pool_send,
    pool_recv,
    all_send,
    all_recv,
):
    me_d, me_p = lax.axis_index("dev"), lax.axis_index("pool")
    requests = table_t.shape[1]
    row_block = hidden.shape[0]
    head_dim = cache.shape[2] // 2
    pair = 2 * head_dim
    width = proj_w.shape[1] // pool_heads
    group = width // head_dim
    half_w = width // 2
    half_g = group // 2
    pack_rows = g_query.shape[1]
    part = pack_rows // 2
    per_dev = requests // devs
    chunks = in_w.shape[1]
    inv_root = 1.0 / math.sqrt(head_dim)

    cache_copies = [
        pltpu.make_async_copy(cache_hbm.at[s], cache.at[s], cache_sem.at[s]) for s in range(slots)
    ]
    for copy in cache_copies:
        copy.start()
    proj_copy = pltpu.make_async_copy(proj_hbm, proj_w, proj_sem.at[0])
    proj_copy.start()

    def in_copy(part_at, c):
        return pltpu.make_async_copy(
            in_hbm.at[part_at, c], in_w.at[part_at, c], in_sem.at[part_at, c]
        )

    def down_copy(c):
        return pltpu.make_async_copy(down_hbm.at[c], down_w.at[c], down_sem.at[c])

    barrier = pltpu.get_barrier_semaphore()
    steps = [(i, j) for i in range(devs) for j in range(pools)][1:]

    def partner(step):
        return {"dev": lax.rem(me_d + step[0], devs), "pool": lax.rem(me_p + step[1], pools)}

    for step in steps:
        pl.semaphore_signal(
            barrier,
            inc=1,
            device_id=partner(step),
            device_id_type=pl.DeviceIdType.MESH,
        )
    pl.semaphore_wait(barrier, len(steps))

    def exchange(axis, me, n, phase, dst):
        send, recv = (dev_send, dev_recv) if axis == "dev" else (pool_send, pool_recv)
        copies = []
        for k in range(1, n):
            peer = lax.rem(me + k, n)
            copies.append(
                pltpu.make_async_remote_copy(
                    src_ref=dst.at[me],
                    dst_ref=dst.at[me],
                    send_sem=send.at[phase, k - 1],
                    recv_sem=recv.at[phase, k - 1],
                    device_id={axis: peer},
                    device_id_type=pl.DeviceIdType.MESH,
                )
            )
            copies[-1].start()
        return copies

    def finish(copies):
        for copy in copies:
            copy.wait()

    count = queries.shape[0]
    q = jnp.concatenate([queries[i].astype(F32) for i in range(count)], axis=0)
    kv = jnp.concatenate([new_keyval[i].astype(F32) for i in range(count)], axis=0)
    left = jnp.concatenate([q[:, :half_w], kv], axis=1)
    right = jnp.concatenate([q[:, half_w:], kv], axis=1)
    g_query[me_d] = jnp.concatenate([left, right], axis=0).astype(BF16)
    sent = exchange("dev", me_d, devs, 0, g_query)

    table = table_t[...].astype(F32)
    rows = slots * group
    first = ((me_d * pools + me_p) * slots).astype(F32)
    row_id = div(iota((rows, 1), 0), group).astype(F32) + first
    len_row = lengths[...].astype(F32)
    cols = devs * pack_rows
    req_at, col_at = iota((requests, cols), 0), iota((requests, cols), 1)
    inner = mod(col_at, part)
    same_request = div(col_at, pack_rows) * per_dev + div(inner, pool_heads) == req_at
    length = jnp.zeros((rows, 1), F32)
    pick = jnp.zeros((rows, cols), F32)
    own_rows = []
    for h in range(pool_heads):
        line = jnp.zeros((1, requests), F32)
        for p in range(pools):
            at = p * pool_heads + h
            line = line + jnp.where(me_p == p, table[at : at + 1, :], 0.0)
        own_rows.append(line)
        mine = jnp.where(line == row_id, 1.0, 0.0)
        length = length + jnp.sum(mine * len_row, axis=1, keepdims=True)
        place = jnp.where(same_request & (mod(inner, pool_heads) == h), 1.0, 0.0)
        pick = pick + dot(mine.astype(BF16), place.astype(BF16))
    row_at, col_at = iota((rows, cols), 0), iota((rows, cols), 1)
    right_half = div(mod(col_at, pack_rows), part) == div(mod(row_at, group), half_g)
    pick = jnp.where(right_half, pick, 0.0).astype(BF16)
    own_g = div(iota((rows, half_w), 1), head_dim) == mod(iota((rows, half_w), 0), half_g)
    fold_at, fold_to = iota((half_w, pair), 0), iota((half_w, pair), 1)
    fold = jnp.where(mod(fold_at, head_dim) == fold_to, 1.0, 0.0).astype(BF16)
    diagonal = iota((requests, requests), 0) == iota((requests, requests), 1)

    def column(line):
        return jnp.sum(jnp.where(diagonal, line, 0.0), axis=1, keepdims=True)

    slot_rows = g_attn.shape[1]
    lane = iota((1, devs * slot_rows), 1)
    lane_slot = mod(lane, slot_rows)
    lane_id = ((div(lane, slot_rows) * pools + me_p) * slots + lane_slot).astype(F32)
    lane_id = jnp.where(lane_slot < slots, lane_id, -1.0)
    attn_picks = [
        jnp.where(column(line) == lane_id, 1.0, 0.0).astype(BF16) for line in own_rows
    ]
    gate_line = jnp.sum(
        jnp.where(ids_t[...] == me_d, gates_t[...], 0.0), axis=0, keepdims=True
    )
    route = column(gate_line)

    finish(sent)
    for c in range(chunks):
        in_copy(0, c).start()
        in_copy(1, c).start()
        down_copy(c).start()

    spread = dot(pick, g_query[...].reshape(cols, g_query.shape[2]))
    query = dot(jnp.where(own_g, spread[:, :half_w], 0.0).astype(BF16), fold)
    fresh = spread[:, half_w : half_w + pair]
    own_score = jnp.sum(query * fresh, axis=1, keepdims=True) * inv_root

    mixed = []
    position = iota((group, cache.shape[1]), 1).astype(F32)
    for s in range(slots):
        cache_copies[s].wait()
        at = slice(s * group, (s + 1) * group)
        entries = cache[s]
        scores = dot_nt(query[at].astype(BF16), entries) * inv_root
        scores = jnp.where(position < length[at], scores, -1e30)
        highest = jnp.maximum(jnp.max(scores, axis=1, keepdims=True), own_score[at])
        raised = jnp.exp(scores - highest)
        own_raised = jnp.exp(own_score[at] - highest)
        scale = 1.0 / (jnp.sum(raised, axis=1, keepdims=True) + own_raised)
        probs = (raised * scale).astype(BF16)
        own_prob = (own_raised * scale).astype(BF16).astype(F32)
        mixed.append(dot(probs, entries) + own_prob * fresh[at])
    mixed = jnp.concatenate(mixed, axis=0)
    values = mixed[:, head_dim:]
    twice = jnp.concatenate([values, values], axis=1)
    wide = jnp.concatenate([twice] * (group // 2), axis=1)
    own_block = div(iota((rows, width), 1), head_dim) == mod(iota((rows, width), 0), group)
    wide = jnp.where(own_block, wide, 0.0).astype(BF16)
    gather = jnp.where(
        div(iota((slot_rows, rows), 1), group) == iota((slot_rows, rows), 0), 1.0, 0.0
    ).astype(BF16)
    g_attn[me_d] = dot(gather, wide).astype(BF16)

    finish_attn = exchange("dev", me_d, devs, 1, g_attn)
    hidden_rows = hidden[...].astype(F32)
    partial = jnp.concatenate(
        [jnp.where(me_p == p, hidden_rows, 0.0) for p in range(pools)], axis=0
    )
    proj_copy.wait()
    finish(finish_attn)
    all_attn = g_attn[...].reshape(devs * slot_rows, width)
    for h in range(pool_heads):
        chosen = dot(attn_picks[h], all_attn).astype(BF16)
        partial = partial + dot_nt(chosen, proj_w[:, h * width : (h + 1) * width])

    pad = g_sum.shape[2] - col_block

    def padded(x):
        if not pad:
            return x
        return jnp.concatenate([x, jnp.zeros((x.shape[0], pad), x.dtype)], axis=1)

    g_sum[me_p] = padded(partial)
    finish(exchange("pool", me_p, pools, 0, g_sum))
    total = g_sum[0]
    for p in range(1, pools):
        total = total + g_sum[p]
    g_resid[me_d] = total.astype(BF16)

    finish(exchange("dev", me_d, devs, 2, g_resid))
    full = jnp.concatenate(
        [g_resid[d].astype(F32)[:, :col_block] for d in range(devs)], axis=1
    )
    mean = jnp.sum(full * full, axis=1, keepdims=True) * (1.0 / full.shape[1])
    normed = (full * lax.rsqrt(mean + 1e-05) * gain[...].reshape(1, -1)).astype(BF16)

    acc[...] = jnp.zeros_like(acc)

    def expert(c, carry):
        in_copy(0, c).wait()
        in_copy(1, c).wait()
        gate = dot_nt(normed, in_w[0, c])
        up = dot_nt(normed, in_w[1, c])
        act = (gate * jax.nn.sigmoid(1.702 * gate) * (up + 1.0)).astype(BF16)
        down_copy(c).wait()
        acc[...] += dot(act, down_w[c])
        return carry

    for c in range(chunks):
        expert(c, 0)
    terms = acc[...] * route
    split = s_moe.shape[3]
    wide_block = g_sum.shape[2]
    for d in range(devs):
        block = padded(terms[:, d * col_block : (d + 1) * col_block])
        for p in range(pools):
            piece = block[p * row_block : (p + 1) * row_block]
            if split < wide_block:
                rest = piece[:, split:]
                fill = jnp.zeros((row_block, 2 * split - wide_block), F32)
                if fill.shape[1]:
                    rest = jnp.concatenate([rest, fill], axis=1)
                piece = jnp.concatenate([piece[:, :split], rest], axis=0)
            s_moe[d, p] = piece.astype(BF16)
    g_moe[me_d, me_p] = s_moe[me_d, me_p]
    copies = []
    for k, step in enumerate(steps):
        target = partner(step)
        copies.append(
            pltpu.make_async_remote_copy(
                src_ref=s_moe.at[target["dev"], target["pool"]],
                dst_ref=g_moe.at[me_d, me_p],
                send_sem=all_send.at[k],
                recv_sem=all_recv.at[k],
                device_id=target,
                device_id_type=pl.DeviceIdType.MESH,
            )
        )
        copies[-1].start()
    resid = g_resid[me_d].astype(F32)
    mine = jnp.zeros((row_block, wide_block), F32)
    for p in range(pools):
        mine = mine + jnp.where(me_p == p, resid[p * row_block : (p + 1) * row_block], 0.0)
    finish(copies)
    summed = jnp.sum(
        g_moe[...].reshape((devs * pools,) + s_moe.shape[2:]).astype(F32), axis=0
    )
    if split < wide_block:
        summed = jnp.concatenate(
            [summed[:row_block], summed[row_block:, : wide_block - split]], axis=1
        )
    out[...] = (mine + summed)[:, :col_block].astype(BF16)


def body(
    devs,
    pools,
    hidden_in,
    queries,
    new_keyval,
    cache_entries,
    slot_table,
    context_len,
    out_proj,
    norm_gain,
    expert_ids,
    expert_gates,
    expert_in,
    expert_down,
):
    slots, context, pair = cache_entries.shape
    requests = slot_table.shape[0]
    pool_heads, width = queries.shape[1:]
    features = norm_gain.shape[0]
    hidden_units = expert_down.shape[1]
    col_block = hidden_in.shape[1]
    col_pad = up_to(col_block, 128)
    part = queries.shape[0] * pool_heads
    chunks = pieces(hidden_units)
    row_block = hidden_in.shape[0]
    moe_block = (row_block, col_pad)
    if row_block % 16:
        moe_block = (2 * row_block, up_to(-(-col_pad // 2), 128))
    slot_rows = up_to(slots, 16)
    depth = hidden_units // chunks
    vmem = pl.BlockSpec(memory_space=pltpu.VMEM)
    hbm = pl.BlockSpec(memory_space=pl.ANY)
    dma = pltpu.SemaphoreType.DMA
    return pl.pallas_call(
        functools.partial(kernel, devs, pools, pool_heads, slots, col_block),
        out_shape=jax.ShapeDtypeStruct(hidden_in.shape, BF16),
        in_specs=[vmem] * 8 + [hbm] * 4,
        out_specs=vmem,
        scratch_shapes=[
            pltpu.VMEM((slots, context, pair), BF16),
            pltpu.VMEM((out_proj.shape[1], out_proj.shape[0]), BF16),
            pltpu.VMEM((2, chunks, depth, features), BF16),
            pltpu.VMEM((chunks, depth, features), BF16),
            pltpu.VMEM((devs, 2 * part, width // 2 + pair), BF16),
            pltpu.VMEM((devs, slot_rows, width), BF16),
            pltpu.VMEM((pools, requests, col_pad), F32),
            pltpu.VMEM((devs, requests, col_pad), BF16),
            pltpu.VMEM((devs, pools) + moe_block, BF16),
            pltpu.VMEM((devs, pools) + moe_block, BF16),
            pltpu.VMEM((requests, features), F32),
            dma((slots,)),
            dma((1,)),
            dma((2, chunks)),
            dma((chunks,)),
            dma((3, devs - 1)),
            dma((3, devs - 1)),
            dma((1, pools - 1)),
            dma((1, pools - 1)),
            dma((devs * pools - 1,)),
            dma((devs * pools - 1,)),
        ],
        compiler_params=pltpu.CompilerParams(
            collective_id=0, has_side_effects=True, vmem_limit_bytes=58 * 2**20
        ),
    )(
        hidden_in,
        queries,
        new_keyval,
        slot_table.T,
        context_len.reshape(1, requests),
        norm_gain,
        expert_ids.T,
        expert_gates.T,
        cache_entries,
        out_proj.T,
        expert_in[0].transpose(1, 2, 0).reshape(2, chunks, depth, features),
        expert_down.reshape(chunks, depth, features),
    )


def solution(mesh):
    return jax.shard_map(
        functools.partial(body, mesh.shape["dev"], mesh.shape["pool"]),
        mesh=mesh,
        in_specs=(
            P(("grp", "pool"), "dev"),
            P(("grp", "dev"), "pool", None),
            P(("grp", "dev"), "pool", None),
            P(("grp", "dev", "pool"), None, None),
            P("grp", None),
            P("grp"),
            P("pool", "dev"),
            P(),
            P("grp", None),
            P("grp", None),
            P("dev", None, None, "pool"),
            P("dev", "pool", None),
        ),
        out_specs=P(("grp", "pool"), "dev"),
        check_vma=False,
    )
```

```python
import functools
import math

import jax
import jax.numpy as jnp
from jax import lax
from jax.experimental import pallas as pl
from jax.experimental.pallas import tpu as pltpu
from jax.sharding import PartitionSpec as P

F32, BF16 = jnp.float32, jnp.bfloat16
NT = (((1,), (1,)), ((), ()))


def up_to(value, step):
    return -(-value // step) * step


def div(x, n):
    if n & (n - 1) == 0:
        return lax.shift_right_logical(x, jnp.full_like(x, n.bit_length() - 1))
    return lax.div(x, jnp.full_like(x, n))


def mod(x, n):
    if n & (n - 1) == 0:
        return x & (n - 1)
    return lax.rem(x, jnp.full_like(x, n))


def iota(shape, dim):
    return lax.broadcasted_iota(jnp.int32, shape, dim)


def pieces(rows):
    for count in (3, 2):
        if rows % count == 0 and (rows // count) % 16 == 0:
            return count
    return 1


def dot(a, b):
    return jnp.dot(a, b, preferred_element_type=F32)


def dot_nt(a, b):
    return lax.dot_general(a, b, NT, preferred_element_type=F32)


def kernel(
    devs,
    pools,
    pool_heads,
    slots,
    col_block,
    hidden,
    queries,
    new_keyval,
    table_t,
    lengths,
    gain,
    ids_t,
    gates_t,
    cache_hbm,
    proj_hbm,
    in_hbm,
    down_hbm,
    out,
    cache,
    proj_w,
    in_w,
    down_w,
    g_query,
    g_attn,
    g_sum,
    g_resid,
    s_moe,
    g_moe,
    acc,
    cache_sem,
    proj_sem,
    in_sem,
    down_sem,
    dev_send,
    dev_recv,
    pool_send,
    pool_recv,
    all_send,
    all_recv,
):
    me_d, me_p = lax.axis_index("dev"), lax.axis_index("pool")
    requests = table_t.shape[1]
    row_block = hidden.shape[0]
    head_dim = cache.shape[2] // 2
    pair = 2 * head_dim
    width = proj_w.shape[1] // pool_heads
    group = width // head_dim
    half_w = width // 2
    half_g = group // 2
    pack_rows = g_query.shape[1]
    part = pack_rows // 2
    per_dev = requests // devs
    chunks = in_w.shape[1]
    inv_root = 1.0 / math.sqrt(head_dim)

    cache_copies = [
        pltpu.make_async_copy(cache_hbm.at[s], cache.at[s], cache_sem.at[s]) for s in range(slots)
    ]
    for copy in cache_copies:
        copy.start()
    proj_copy = pltpu.make_async_copy(proj_hbm, proj_w, proj_sem.at[0])
    proj_copy.start()

    def in_copy(part_at, c):
        return pltpu.make_async_copy(
            in_hbm.at[part_at, c], in_w.at[part_at, c], in_sem.at[part_at, c]
        )

    def down_copy(c):
        return pltpu.make_async_copy(down_hbm.at[c], down_w.at[c], down_sem.at[c])

    barrier = pltpu.get_barrier_semaphore()
    steps = [(i, j) for i in range(devs) for j in range(pools)][1:]

    def partner(step):
        return {"dev": lax.rem(me_d + step[0], devs), "pool": lax.rem(me_p + step[1], pools)}

    for step in steps:
        pl.semaphore_signal(
            barrier,
            inc=1,
            device_id=partner(step),
            device_id_type=pl.DeviceIdType.MESH,
        )
    pl.semaphore_wait(barrier, len(steps))

    def exchange(axis, me, n, phase, dst):
        send, recv = (dev_send, dev_recv) if axis == "dev" else (pool_send, pool_recv)
        copies = []
        for k in range(1, n):
            peer = lax.rem(me + k, n)
            copies.append(
                pltpu.make_async_remote_copy(
                    src_ref=dst.at[me],
                    dst_ref=dst.at[me],
                    send_sem=send.at[phase, k - 1],
                    recv_sem=recv.at[phase, k - 1],
                    device_id={axis: peer},
                    device_id_type=pl.DeviceIdType.MESH,
                )
            )
            copies[-1].start()
        return copies

    def finish(copies):
        for copy in copies:
            copy.wait()

    count = queries.shape[0]
    q = jnp.concatenate([queries[i].astype(F32) for i in range(count)], axis=0)
    kv = jnp.concatenate([new_keyval[i].astype(F32) for i in range(count)], axis=0)
    left = jnp.concatenate([q[:, :half_w], kv], axis=1)
    right = jnp.concatenate([q[:, half_w:], kv], axis=1)
    g_query[me_d] = jnp.concatenate([left, right], axis=0).astype(BF16)
    sent = exchange("dev", me_d, devs, 0, g_query)

    table = table_t[...].astype(F32)
    rows = slots * group
    first = ((me_d * pools + me_p) * slots).astype(F32)
    row_id = div(iota((rows, 1), 0), group).astype(F32) + first
    len_row = lengths[...].astype(F32)
    cols = devs * pack_rows
    req_at, col_at = iota((requests, cols), 0), iota((requests, cols), 1)
    inner = mod(col_at, part)
    same_request = div(col_at, pack_rows) * per_dev + div(inner, pool_heads) == req_at
    length = jnp.zeros((rows, 1), F32)
    pick = jnp.zeros((rows, cols), F32)
    own_rows = []
    for h in range(pool_heads):
        line = jnp.zeros((1, requests), F32)
        for p in range(pools):
            at = p * pool_heads + h
            line = line + jnp.where(me_p == p, table[at : at + 1, :], 0.0)
        own_rows.append(line)
        mine = jnp.where(line == row_id, 1.0, 0.0)
        length = length + jnp.sum(mine * len_row, axis=1, keepdims=True)
        place = jnp.where(same_request & (mod(inner, pool_heads) == h), 1.0, 0.0)
        pick = pick + dot(mine.astype(BF16), place.astype(BF16))
    row_at, col_at = iota((rows, cols), 0), iota((rows, cols), 1)
    right_half = div(mod(col_at, pack_rows), part) == div(mod(row_at, group), half_g)
    pick = jnp.where(right_half, pick, 0.0).astype(BF16)
    own_g = div(iota((rows, half_w), 1), head_dim) == mod(iota((rows, half_w), 0), half_g)
    fold_at, fold_to = iota((half_w, pair), 0), iota((half_w, pair), 1)
    fold = jnp.where(mod(fold_at, head_dim) == fold_to, 1.0, 0.0).astype(BF16)
    diagonal = iota((requests, requests), 0) == iota((requests, requests), 1)

    def column(line):
        return jnp.sum(jnp.where(diagonal, line, 0.0), axis=1, keepdims=True)

    slot_rows = g_attn.shape[1]
    lane = iota((1, devs * slot_rows), 1)
    lane_slot = mod(lane, slot_rows)
    lane_id = ((div(lane, slot_rows) * pools + me_p) * slots + lane_slot).astype(F32)
    lane_id = jnp.where(lane_slot < slots, lane_id, -1.0)
    attn_picks = [
        jnp.where(column(line) == lane_id, 1.0, 0.0).astype(BF16) for line in own_rows
    ]
    gate_line = jnp.sum(
        jnp.where(ids_t[...] == me_d, gates_t[...], 0.0), axis=0, keepdims=True
    )
    route = column(gate_line)

    finish(sent)
    for c in range(chunks):
        in_copy(0, c).start()
        in_copy(1, c).start()
        down_copy(c).start()

    spread = dot(pick, g_query[...].reshape(cols, g_query.shape[2]))
    query = dot(jnp.where(own_g, spread[:, :half_w], 0.0).astype(BF16), fold)
    fresh = spread[:, half_w : half_w + pair]
    own_score = jnp.sum(query * fresh, axis=1, keepdims=True) * inv_root

    mixed = []
    position = iota((group, cache.shape[1]), 1).astype(F32)
    for s in range(slots):
        cache_copies[s].wait()
        at = slice(s * group, (s + 1) * group)
        entries = cache[s]
        scores = dot_nt(query[at].astype(BF16), entries) * inv_root
        scores = jnp.where(position < length[at], scores, -1e30)
        highest = jnp.maximum(jnp.max(scores, axis=1, keepdims=True), own_score[at])
        raised = jnp.exp(scores - highest)
        own_raised = jnp.exp(own_score[at] - highest)
        scale = 1.0 / (jnp.sum(raised, axis=1, keepdims=True) + own_raised)
        probs = (raised * scale).astype(BF16)
        own_prob = (own_raised * scale).astype(BF16).astype(F32)
        mixed.append(dot(probs, entries) + own_prob * fresh[at])
    mixed = jnp.concatenate(mixed, axis=0)
    values = mixed[:, head_dim:]
    twice = jnp.concatenate([values, values], axis=1)
    wide = jnp.concatenate([twice] * (group // 2), axis=1)
    own_block = div(iota((rows, width), 1), head_dim) == mod(iota((rows, width), 0), group)
    wide = jnp.where(own_block, wide, 0.0).astype(BF16)
    gather = jnp.where(
        div(iota((slot_rows, rows), 1), group) == iota((slot_rows, rows), 0), 1.0, 0.0
    ).astype(BF16)
    g_attn[me_d] = dot(gather, wide).astype(BF16)

    finish_attn = exchange("dev", me_d, devs, 1, g_attn)
    hidden_rows = hidden[...].astype(F32)
    partial = jnp.concatenate(
        [jnp.where(me_p == p, hidden_rows, 0.0) for p in range(pools)], axis=0
    )
    proj_copy.wait()
    finish(finish_attn)
    all_attn = g_attn[...].reshape(devs * slot_rows, width)
    for h in range(pool_heads):
        chosen = dot(attn_picks[h], all_attn).astype(BF16)
        partial = partial + dot_nt(chosen, proj_w[:, h * width : (h + 1) * width])

    pad = g_sum.shape[2] - col_block

    def padded(x):
        if not pad:
            return x
        return jnp.concatenate([x, jnp.zeros((x.shape[0], pad), x.dtype)], axis=1)

    g_sum[me_p] = padded(partial)
    finish(exchange("pool", me_p, pools, 0, g_sum))
    total = g_sum[0]
    for p in range(1, pools):
        total = total + g_sum[p]
    g_resid[me_d] = total.astype(BF16)

    finish(exchange("dev", me_d, devs, 2, g_resid))
    full = jnp.concatenate(
        [g_resid[d].astype(F32)[:, :col_block] for d in range(devs)], axis=1
    )
    mean = jnp.sum(full * full, axis=1, keepdims=True) * (1.0 / full.shape[1])
    normed = (full * lax.rsqrt(mean + 1e-05) * gain[...].reshape(1, -1)).astype(BF16)

    acc[...] = jnp.zeros_like(acc)

    def expert(c, carry):
        in_copy(0, c).wait()
        in_copy(1, c).wait()
        gate = dot_nt(normed, in_w[0, c])
        up = dot_nt(normed, in_w[1, c])
        act = (gate * jax.nn.sigmoid(1.702 * gate) * (up + 1.0)).astype(BF16)
        down_copy(c).wait()
        acc[...] += dot(act, down_w[c])
        return carry

    for c in range(chunks):
        expert(c, 0)
    terms = acc[...] * route
    split = s_moe.shape[3]
    wide_block = g_sum.shape[2]
    for d in range(devs):
        block = padded(terms[:, d * col_block : (d + 1) * col_block])
        for p in range(pools):
            piece = block[p * row_block : (p + 1) * row_block]
            if split < wide_block:
                rest = piece[:, split:]
                fill = jnp.zeros((row_block, 2 * split - wide_block), F32)
                if fill.shape[1]:
                    rest = jnp.concatenate([rest, fill], axis=1)
                piece = jnp.concatenate([piece[:, :split], rest], axis=0)
            s_moe[d, p] = piece.astype(BF16)
    g_moe[me_d, me_p] = s_moe[me_d, me_p]
    copies = []
    for k, step in enumerate(steps):
        target = partner(step)
        copies.append(
            pltpu.make_async_remote_copy(
                src_ref=s_moe.at[target["dev"], target["pool"]],
                dst_ref=g_moe.at[me_d, me_p],
                send_sem=all_send.at[k],
                recv_sem=all_recv.at[k],
                device_id=target,
                device_id_type=pl.DeviceIdType.MESH,
            )
        )
        copies[-1].start()
    resid = g_resid[me_d].astype(F32)
    mine = jnp.zeros((row_block, wide_block), F32)
    for p in range(pools):
        mine = mine + jnp.where(me_p == p, resid[p * row_block : (p + 1) * row_block], 0.0)
    finish(copies)
    summed = jnp.sum(
        g_moe[...].reshape((devs * pools,) + s_moe.shape[2:]).astype(F32), axis=0
    )
    if split < wide_block:
        summed = jnp.concatenate(
            [summed[:row_block], summed[row_block:, : wide_block - split]], axis=1
        )
    out[...] = (mine + summed)[:, :col_block].astype(BF16)


def body(
    devs,
    pools,
    hidden_in,
    queries,
    new_keyval,
    cache_entries,
    slot_table,
    context_len,
    out_proj,
    norm_gain,
    expert_ids,
    expert_gates,
    expert_in,
    expert_down,
):
    slots, context, pair = cache_entries.shape
    requests = slot_table.shape[0]
    pool_heads, width = queries.shape[1:]
    features = norm_gain.shape[0]
    hidden_units = expert_down.shape[1]
    col_block = hidden_in.shape[1]
    col_pad = up_to(col_block, 128)
    part = queries.shape[0] * pool_heads
    chunks = pieces(hidden_units)
    row_block = hidden_in.shape[0]
    moe_block = (row_block, col_pad)
    if row_block % 16:
        moe_block = (2 * row_block, up_to(-(-col_pad // 2), 128))
    slot_rows = up_to(slots, 16)
    depth = hidden_units // chunks
    vmem = pl.BlockSpec(memory_space=pltpu.VMEM)
    hbm = pl.BlockSpec(memory_space=pl.ANY)
    dma = pltpu.SemaphoreType.DMA
    return pl.pallas_call(
        functools.partial(kernel, devs, pools, pool_heads, slots, col_block),
        out_shape=jax.ShapeDtypeStruct(hidden_in.shape, BF16),
        in_specs=[vmem] * 8 + [hbm] * 4,
        out_specs=vmem,
        scratch_shapes=[
            pltpu.VMEM((slots, context, pair), BF16),
            pltpu.VMEM((out_proj.shape[1], out_proj.shape[0]), BF16),
            pltpu.VMEM((2, chunks, depth, features), BF16),
            pltpu.VMEM((chunks, depth, features), BF16),
            pltpu.VMEM((devs, 2 * part, width // 2 + pair), BF16),
            pltpu.VMEM((devs, slot_rows, width), BF16),
            pltpu.VMEM((pools, requests, col_pad), F32),
            pltpu.VMEM((devs, requests, col_pad), BF16),
            pltpu.VMEM((devs, pools) + moe_block, BF16),
            pltpu.VMEM((devs, pools) + moe_block, BF16),
            pltpu.VMEM((requests, features), F32),
            dma((slots,)),
            dma((1,)),
            dma((2, chunks)),
            dma((chunks,)),
            dma((3, devs - 1)),
            dma((3, devs - 1)),
            dma((1, pools - 1)),
            dma((1, pools - 1)),
            dma((devs * pools - 1,)),
            dma((devs * pools - 1,)),
        ],
        compiler_params=pltpu.CompilerParams(
            collective_id=0, has_side_effects=True, vmem_limit_bytes=58 * 2**20
        ),
    )(
        hidden_in,
        queries,
        new_keyval,
        slot_table.T,
        context_len.reshape(1, requests),
        norm_gain,
        expert_ids.T,
        expert_gates.T,
        cache_entries,
        out_proj.T,
        expert_in[0].transpose(1, 2, 0).reshape(2, chunks, depth, features),
        expert_down.reshape(chunks, depth, features),
    )


def solution(mesh):
    return jax.shard_map(
        functools.partial(body, mesh.shape["dev"], mesh.shape["pool"]),
        mesh=mesh,
        in_specs=(
            P(("grp", "pool"), "dev"),
            P(("grp", "dev"), "pool", None),
            P(("grp", "dev"), "pool", None),
            P(("grp", "dev", "pool"), None, None),
            P("grp", None),
            P("grp"),
            P("pool", "dev"),
            P(),
            P("grp", None),
            P("grp", None),
            P("dev", None, None, "pool"),
            P("dev", "pool", None),
        ),
        out_specs=P(("grp", "pool"), "dev"),
        check_vma=False,
    )
```
